32 devices in a mesh: gx: 16 (over z, y, core), gy: 2 (over x).
Axes of the slice: x: 2, y: 2, z: 4, core: 2. Of those that a mesh axis runs over, the one named last changes fastest.
Arguments:
- positions: float32 [3, 4096], P(None, ('gx', 'gy')), as said below
- species: int32 [4096], P(('gx', 'gy')), may hold values from 0 to 5
- neighbours: int32 [64, 4096], P(None, ('gx', 'gy')), may hold values from 0 to 512, as said below
- face_sends: int32 [4, 2048], P(None, ('gx', 'gy')), may hold values from 0 to 127, as said below
- corner_sends: int32 [4, 1024], P(None, ('gx', 'gy')), may hold values from 0 to 127, as said below
- embed: float32 [6, 128], replicated, may hold values from -6 to 6
- radial: float32 [2, 8, 128], replicated, may hold values from -6 to 6
- w_up: float32 [128, 128], replicated, may hold values from -0.5 to 0.5
- w_charge: float32 [128, 128], replicated, may hold values from -0.5 to 0.5
- kvec: float32 [3, 2048], replicated, may hold values from -4 to 4
- kfilter: float32 [2048, 128], replicated, may hold values from -6 to 6
- read: float32 [128], replicated, may hold values from -0.5 to 0.5
Outputs:
- atom_energy: float32 [4096], P(('gx', 'gy'))
- forces: float32 [3, 4096], P(None, ('gx', 'gy'))
- grad_embed: float32 [6, 128], replicated
- grad_radial: float32 [2, 8, 128], replicated
- grad_up: float32 [128, 128], replicated
- grad_charge: float32 [128, 128], replicated
- grad_filter: float32 [2048, 128], replicated
- grad_read: float32 [128], replicated
The draws below stay inside these ranges and needn't reach their ends.
Inputs may be any that keep to these rules, and one draw needn't show every extreme that they name: `positions`: each domain is 8.8 wide along the first two dimensions; coordinates are relative to its corner. `neighbours`: entry [s, i] names a slot of atom i's device's extended list: 0 to 127 are its own atoms in order, then 64 atoms for each face direction and 32 for each corner direction, in the order of the steps; the value 128 + 6 * 64 marks an empty slot. An atom never names itself. `face_sends`: row f of a device lists 64 of its own atoms for face direction f; every own atom appears in some row. `corner_sends`: row f of a device lists 64 / 2 of its own atoms for corner direction f; every own atom appears in some row.
All inputs are finite; a program needn't handle non-finite values.
Results may differ from the reference program's by a relative error of at most 0.0003.
Values sent between devices are 32-bit elements; how exact they have to be, the bound alone decides.
A program may use at most 64 MiB of HBM per device.

```python
import math
import jax
import jax.numpy as jnp
import numpy as np
from jax import lax

C = 128
RADIAL = 8
SPECIES = 6
KVEC = 2048
NBR = 64
ATOM_DEV = 128
HALO = 64
ATOMS = 4096
N_GX = 16
N_GY = 2


def offset_table():
    found = []
    for step_x in range(-2, 3):
        for step_y in range(-2, 3):
            for step_z in range(-2, 3):
                norm_sq = step_x * step_x + step_y * step_y + step_z * step_z
                if 0 < norm_sq <= 5:
                    found.append((step_x, step_y, step_z))
    return np.array(found, dtype=np.int32)


def lattice_layout(key):
    devices = N_GX * N_GY
    keys = jax.random.split(key, devices)
    site_of = jax.vmap(lambda sub: jax.random.permutation(sub, ATOM_DEV))(keys).astype(jnp.int32)
    slot_of = jnp.argsort(site_of, axis=1).astype(jnp.int32)
    return (site_of, slot_of)


def draw_positions(key, part):
    site_of, slot_of = lattice_layout(key)
    key = jax.random.fold_in(key, 7)
    depth = ATOM_DEV // 16
    site_x = site_of // (4 * depth)
    site_y = site_of // depth % 4
    site_z = site_of % depth
    lattice = jnp.stack([site_x, site_y, site_z]).astype(jnp.float32) * 2.2 + 1.1
    jitter = jax.random.uniform(key, lattice.shape, jnp.float32, -0.3, 0.3)
    return (lattice + jitter).reshape(3, -1)


def draw_neighbours(key, part):
    site_of, slot_of = lattice_layout(key)
    key = jax.random.fold_in(key, 8)
    devices = N_GX * N_GY
    depth = ATOM_DEV // 16
    half = ATOM_DEV // 2
    quarter = ATOM_DEV // 4
    empty = ATOM_DEV + 6 * half
    offsets = jnp.asarray(offset_table())
    site_x = (site_of // (4 * depth))[..., None]
    site_y = (site_of // depth % 4)[..., None]
    site_z = (site_of % depth)[..., None]
    target_x = site_x + offsets[:, 0]
    target_y = site_y + offsets[:, 1]
    target_z = site_z + offsets[:, 2]
    move_x = (target_x >= 4).astype(jnp.int32) - (target_x < 0).astype(jnp.int32)
    move_y = (target_y >= 4).astype(jnp.int32) - (target_y < 0).astype(jnp.int32)
    wrap_x = target_x - 4 * move_x
    wrap_y = target_y - 4 * move_y
    inside = (target_z >= 0) & (target_z < depth)
    clip_z = jnp.clip(target_z, 0, depth - 1)
    near_x = jnp.where(move_x == 1, wrap_x, wrap_x - 2)
    near_y = jnp.where(move_y == 1, wrap_y, wrap_y - 2)
    own_site = (wrap_x * 4 + wrap_y) * depth + clip_z
    own_slot = jnp.take_along_axis(slot_of, own_site.reshape(devices, -1), axis=1).reshape(own_site.shape)
    face_x = ATOM_DEV + jnp.where(move_x == 1, 0, 1) * half + (near_x * 4 + wrap_y) * depth + clip_z
    face_y = ATOM_DEV + jnp.where(move_y == 1, 2, 3) * half + (wrap_x * 2 + near_y) * depth + clip_z
    corner_num = 2 * (move_x == -1).astype(jnp.int32) + (move_y == -1).astype(jnp.int32)
    corner = ATOM_DEV + 4 * half + corner_num * quarter + (near_x * 2 + near_y) * depth + clip_z
    entry = jnp.where((move_x == 0) & (move_y == 0), own_slot, jnp.where(move_y == 0, face_x, jnp.where(move_x == 0, face_y, corner)))
    entry = jnp.where(inside, entry, empty)
    padding = jnp.full(entry.shape[:2] + (NBR - offsets.shape[0],), empty, jnp.int32)
    entry = jnp.concatenate([entry.astype(jnp.int32), padding], axis=2)
    rolls = jax.random.randint(key, entry.shape[:2] + (1,), 0, NBR)
    columns = (jnp.arange(NBR, dtype=jnp.int32)[None, None, :] + rolls) % NBR
    entry = jnp.take_along_axis(entry, columns, axis=2)
    return entry.transpose(2, 0, 1).reshape(NBR, -1)


def draw_face_sends(key, part):
    site_of, slot_of = lattice_layout(key)
    depth = ATOM_DEV // 16
    half = ATOM_DEV // 2
    place = jnp.arange(half, dtype=jnp.int32)
    layer_z = place % depth
    deep_x = place // (4 * depth)
    across_y = place // depth % 4
    across_x = place // (2 * depth)
    deep_y = place // depth % 2
    rows = jnp.stack([(deep_x * 4 + across_y) * depth + layer_z, ((deep_x + 2) * 4 + across_y) * depth + layer_z, (across_x * 4 + deep_y) * depth + layer_z, (across_x * 4 + deep_y + 2) * depth + layer_z])
    slots = slot_of[:, rows]
    return slots.transpose(1, 0, 2).reshape(4, -1)


def draw_corner_sends(key, part):
    site_of, slot_of = lattice_layout(key)
    depth = ATOM_DEV // 16
    quarter = ATOM_DEV // 4
    place = jnp.arange(quarter, dtype=jnp.int32)
    layer_z = place % depth
    deep_x = place // (2 * depth)
    deep_y = place // depth % 2
    rows = jnp.stack([(deep_x * 4 + deep_y) * depth + layer_z, (deep_x * 4 + deep_y + 2) * depth + layer_z, ((deep_x + 2) * 4 + deep_y) * depth + layer_z, ((deep_x + 2) * 4 + deep_y + 2) * depth + layer_z])
    slots = slot_of[:, rows]
    return slots.transpose(1, 0, 2).reshape(4, -1)


def place_ends(entries, stream_key, least, largest):
    index_at = [jax.random.randint(jax.random.fold_in(stream_key, axis), (), 0, length) for axis, length in enumerate(entries.shape)]
    widest = entries.shape.index(max(entries.shape))
    neighbour = index_at[:widest] + [(index_at[widest] + 1) % entries.shape[widest]] + index_at[widest + 1:]
    return entries.at[tuple(index_at)].set(least).at[tuple(neighbour)].set(largest)


def noise(stream_key, dims, spread, most, held_as=jnp.bfloat16):
    return jnp.clip(spread * jax.random.normal(stream_key, dims, jnp.float32), -most, most).astype(held_as)


def setup_inputs(seed: int = 0) -> dict:
    streams_of = jax.random.split(jax.random.key(seed), 13)
    positions = draw_positions(jax.random.fold_in(streams_of[12], 71), 0)
    species = place_ends(jax.random.randint(streams_of[1], (ATOMS,), 0, SPECIES), jax.random.fold_in(streams_of[1], 1), 0, SPECIES - 1).astype(jnp.int32)
    neighbours = draw_neighbours(jax.random.fold_in(streams_of[12], 71), 0)
    face_sends = draw_face_sends(jax.random.fold_in(streams_of[12], 71), 0)
    corner_sends = draw_corner_sends(jax.random.fold_in(streams_of[12], 71), 0)
    embed = noise(streams_of[5], (SPECIES, C), 1.0, 6.0, jnp.float32)
    radial = noise(streams_of[6], (2, RADIAL, C), 1.0, 6.0, jnp.float32)
    w_up = noise(streams_of[7], (C, C), C ** -0.5, 0.5, jnp.float32)
    w_charge = noise(streams_of[8], (C, C), C ** -0.5, 0.5, jnp.float32)
    kvec = noise(streams_of[9], (3, KVEC), 0.5, 4.0, jnp.float32)
    kfilter = noise(streams_of[10], (KVEC, C), 1.0, 6.0, jnp.float32)
    read = noise(streams_of[11], (C,), C ** -0.5, 0.5, jnp.float32)
    return dict(positions=positions, species=species, neighbours=neighbours, face_sends=face_sends, corner_sends=corner_sends, embed=embed, radial=radial, w_up=w_up, w_charge=w_charge, kvec=kvec, kfilter=kfilter, read=read)


CUTOFF = 5.0
SOFTEN = 0.01
WIDTH_GAUSS = 2.0
NORMALIZE = 4.0
DOMAIN = 8.8
slot_group = 16
HIGHEST = lax.Precision.HIGHEST
FACE_DIRS = ((1, 0), (-1, 0), (0, 1), (0, -1))
CORNER_DIRS = ((1, 1), (1, -1), (-1, 1), (-1, -1))

def product(left, right):
    return jnp.dot(left, right, precision=HIGHEST, preferred_element_type=jnp.float32)

def edge_block(coords, ext_pos, ext_feat, weights, centers, slots):
    limit = ext_pos.shape[1]
    valid = (slots < limit).astype(jnp.float32)
    index = jnp.minimum(slots, limit - 1)
    offset_vec = ext_pos[:, index] - coords[:, None, :]
    dist_sq = lax.optimization_barrier(jnp.sum(offset_vec * offset_vec, axis=0))
    radius = jnp.sqrt(dist_sq + SOFTEN)
    envelope = jnp.square(jnp.maximum(1.0 - dist_sq / (CUTOFF * CUTOFF), 0.0)) * valid
    basis = jnp.exp(-WIDTH_GAUSS * jnp.square(radius[None] - centers[:, None, None])) * envelope[None]
    radial_zero = jnp.einsum('bc,bsa->csa', weights[0], basis, precision=HIGHEST)
    radial_one = jnp.einsum('bc,bsa->csa', weights[1], basis, precision=HIGHEST)
    gathered = ext_feat[:, index]
    scalar_part = lax.optimization_barrier(jnp.sum(radial_zero * gathered, axis=1))
    vector_part = jnp.einsum('csa,dsa->dca', radial_one * gathered, offset_vec, precision=HIGHEST)
    return (scalar_part, vector_part)

def edge_features(coords, halo_pos, features, halo_feat, weights, neighbours):
    ext_pos = jnp.concatenate([coords, halo_pos], axis=1)
    ext_feat = jnp.concatenate([features, halo_feat], axis=1)
    basis_count = weights.shape[1]
    centers = jnp.arange(basis_count, dtype=jnp.float32) * (CUTOFF / (basis_count - 1))
    channels = features.shape[0]
    atoms = coords.shape[1]
    groups = neighbours.reshape(-1, slot_group, atoms)
    blocked = jax.checkpoint(edge_block)

    def step(carry, slots):
        first, second = blocked(coords, ext_pos, ext_feat, weights, centers, slots)
        return ((carry[0] + first, carry[1] + second), None)
    start = (jnp.zeros((channels, atoms), jnp.float32), jnp.zeros((3, channels, atoms), jnp.float32))
    (scalar_msg, vector_msg), _ = lax.scan(step, start, groups)
    scalar_msg = scalar_msg / NORMALIZE
    vector_msg = vector_msg / (NORMALIZE * CUTOFF)
    return scalar_msg + lax.optimization_barrier(jnp.sum(jnp.square(vector_msg), axis=0))

def phase_block(global_pos, k_block):
    phase_angle = k_block[0][:, None] * global_pos[0][None, :] + k_block[1][:, None] * global_pos[1][None, :] + k_block[2][:, None] * global_pos[2][None, :]
    return (jnp.cos(phase_angle), jnp.sin(phase_angle))

def reference(positions, species, neighbours, face_sends, corner_sends, embed, radial, w_up, w_charge, kvec, kfilter, read):
    devices = N_GX * N_GY
    pos_dev = positions.reshape(3, devices, ATOM_DEV).transpose(1, 0, 2)
    nbr_dev = neighbours.reshape(NBR, devices, ATOM_DEV).transpose(1, 0, 2)
    face_dev = face_sends.reshape(4, devices, HALO).transpose(1, 0, 2)
    corner_dev = corner_sends.reshape(4, devices, HALO // 2).transpose(1, 0, 2)
    spec_dev = species.reshape(devices, ATOM_DEV)
    dev_ids = jnp.arange(devices, dtype=jnp.int32)
    scale = 1.0 / math.sqrt(ATOMS * KVEC)

    def global_pos(device, coords):
        row_index = (device // N_GY).astype(jnp.float32)
        col_index = (device % N_GY).astype(jnp.float32)
        anchor = jnp.stack([row_index * DOMAIN, col_index * DOMAIN, jnp.zeros((), jnp.float32)])
        return coords + anchor[:, None]

    def energies(pos_dev, embed, radial, w_up, w_charge, kfilter, read):
        onehot = (spec_dev[:, None, :] == jnp.arange(SPECIES, dtype=jnp.int32)[None, :, None]).astype(jnp.float32)
        initial_dev = jnp.einsum('sc,dsa->dca', embed, onehot, precision=HIGHEST)
        source = jnp.concatenate([pos_dev, initial_dev], axis=1)

        def short_range(items):
            device, coords, slots = items
            row_index = device // N_GY
            col_index = device % N_GY
            pieces = []
            for table, directions in ((face_dev, FACE_DIRS), (corner_dev, CORNER_DIRS)):
                for number, (step_x, step_y) in enumerate(directions):
                    other = (row_index + step_x) % N_GX * N_GY + (col_index + step_y) % N_GY
                    piece = source[other][:, table[other, number]]
                    shift_vec = jnp.array([step_x * DOMAIN, step_y * DOMAIN, 0.0], dtype=jnp.float32)[:, None]
                    pieces.append(jnp.concatenate([piece[:3] + shift_vec, piece[3:]], axis=0))
            halo_rows = jnp.concatenate(pieces, axis=1)
            initial = initial_dev[device]
            invariants = edge_features(coords, halo_rows[:3], initial, halo_rows[3:], radial, slots)
            updated = initial + product(w_up.T, jax.nn.silu(invariants))
            charges = product(w_charge.T, updated)
            return (updated, charges)
        updated_dev, charge_dev = lax.map(jax.checkpoint(short_range), (dev_ids, pos_dev, nbr_dev))

        def accumulate(total, items):
            device, coords, charges = items
            cosine, sine = phase_block(global_pos(device, coords), kvec)
            return ((total[0] + product(cosine, charges.T), total[1] + product(sine, charges.T)), None)
        start = (jnp.zeros((KVEC, C), jnp.float32), jnp.zeros((KVEC, C), jnp.float32))
        (cos_factor, sin_factor), _ = lax.scan(jax.checkpoint(accumulate), start, (dev_ids, pos_dev, charge_dev))

        def long_range(items):
            device, coords, updated = items
            cosine, sine = phase_block(global_pos(device, coords), kvec)
            potential = scale * (product((kfilter * cos_factor).T, cosine) + product((kfilter * sin_factor).T, sine))
            combined = updated + potential
            return product(read[None, :], jax.nn.silu(combined))[0]
        return lax.map(jax.checkpoint(long_range), (dev_ids, pos_dev, updated_dev))
    energy_dev, pullback = jax.vjp(energies, pos_dev, embed, radial, w_up, w_charge, kfilter, read)
    grads = pullback(jnp.ones_like(energy_dev))
    grad_pos, grad_embed, grad_radial, grad_up, grad_charge, grad_filter, grad_read = grads
    atom_energy = energy_dev.reshape(ATOMS)
    forces = -grad_pos.transpose(1, 0, 2).reshape(3, ATOMS)
    return (atom_energy, forces, grad_embed / ATOMS, grad_radial / ATOMS, grad_up / ATOMS, grad_charge / ATOMS, grad_filter, grad_read / ATOMS)
```

```python
import functools
import math

import jax
import jax.numpy as jnp
import numpy as np
from jax import lax
from jax.experimental import pallas as pl
from jax.experimental.pallas import tpu as pltpu
from jax.sharding import PartitionSpec as P

CUTOFF = 5.0
SOFTEN = 0.01
DOMAIN = 8.8
HIGH = lax.Precision.HIGH
MESH = pl.DeviceIdType.MESH
DIRS = ((1, 0), (-1, 0), (0, 1), (0, -1), (1, 1), (1, -1), (-1, 1), (-1, -1))


def turn_tables():
    grid = 0.5 * np.cos(np.pi * (np.arange(400) + 0.5) / 400)
    grid = grid[grid > 0]
    square = grid * grid
    powers = np.stack([square**n for n in range(9)], axis=1)
    sine = np.linalg.lstsq(powers[:, :8], np.sin(2 * np.pi * grid) / grid, rcond=None)[0]
    cosine = np.linalg.lstsq(powers, np.cos(2 * np.pi * grid), rcond=None)[0]
    return [float(np.float32(v)) for v in sine], [float(np.float32(v)) for v in cosine]


SIN_TABLE, COS_TABLE = turn_tables()


def cos_sin(turns):
    part = turns - jnp.round(turns)
    square = part * part
    sine = jnp.full_like(part, SIN_TABLE[-1])
    for value in SIN_TABLE[-2::-1]:
        sine = sine * square + value
    cosine = jnp.full_like(part, COS_TABLE[-1])
    for value in COS_TABLE[-2::-1]:
        cosine = cosine * square + value
    return cosine, sine * part


def mm(spec, left, right):
    return jnp.einsum(spec, left, right, precision=HIGH, preferred_element_type=jnp.float32)


def gather_kernel(n_gx, n_gy, x_ref, out_ref, send_sem, recv_sem):
    rows = x_ref.shape[0]
    first = (rows // 2 + 7) // 8 * 8
    line = n_gx // 4
    gx = lax.axis_index("gx")
    gy = lax.axis_index("gy")
    at = gx // 4
    mid = gx // 2 % 2
    core = gx % 2
    used = [0]
    started = []

    def slot(z, m, c, b):
        return (z * 4 + m * 2 + c) * n_gy + b

    def whole(index):
        return out_ref.at[index]

    def head(index):
        return out_ref.at[index, pl.ds(0, first)]

    def tail(index):
        return out_ref.at[index, pl.ds(first, rows - first)]

    def push(view, index, half, device, cond):
        number = used[0]
        used[0] += 1

        def make():
            return pltpu.make_async_remote_copy(
                src_ref=view(index),
                dst_ref=view(index),
                send_sem=send_sem.at[number],
                recv_sem=recv_sem.at[index, half],
                device_id=device,
                device_id_type=MESH,
            )

        make().start()
        started.append((cond, make))

    def arrive(view, index, half):
        pltpu.make_async_copy(view(index), view(index), recv_sem.at[index, half]).wait()

    def device(z, m, c, b):
        return (z * 4 + m * 2 + c, b)

    def guarded(cond, function):
        if cond is None:
            function()
        else:
            pl.when(cond)(function)

    barrier = pltpu.get_barrier_semaphore()
    others = [lax.rem(gy + step, n_gy) for step in range(1, n_gy)]

    def greet(target):
        pl.semaphore_signal(barrier, inc=1, device_id=target, device_id_type=MESH)

    pl.when(at > 0)(lambda: greet(device(at - 1, mid, core, gy)))
    pl.when(at < line - 1)(lambda: greet(device(at + 1, mid, core, gy)))
    greet(device(at, 1 - mid, core, gy))
    greet(device(at, mid, 1 - core, gy))
    for other in others:
        greet(device(at, mid, core, other))
    out_ref[slot(at, mid, core, gy)] = x_ref[...]
    inner = (at > 0) & (at < line - 1)
    pl.when(inner)(lambda: pl.semaphore_wait(barrier, 3 + n_gy))
    pl.when(jnp.logical_not(inner))(lambda: pl.semaphore_wait(barrier, 2 + n_gy))

    above, below = device(at + 1, mid, core, gy), device(at - 1, mid, core, gy)
    across_to, core_to = device(at, 1 - mid, core, gy), device(at, mid, 1 - core, gy)
    beside_to = [device(at, mid, core, other) for other in others]

    def stage_one(cond, z, kind):
        own = slot(z, mid, core, gy)
        up = (at < line - 1) if cond is None else cond & (at < line - 1)
        down = (at > 0) if cond is None else cond & (at > 0)
        if kind != 0:
            guarded(cond, lambda: arrive(whole, own, 0))
        if kind >= 0:
            guarded(up, lambda: push(whole, own, 0, above, up))
        if kind <= 0:
            guarded(down, lambda: push(whole, own, 0, below, down))

        def spread():
            push(whole, own, 0, across_to, cond)
            for target in beside_to:
                push(whole, own, 0, target, cond)
            push(whole, own, 0, core_to, cond)

        guarded(cond, spread)

    def stage_two(cond, z):
        across = slot(z, 1 - mid, core, gy)
        beside = [slot(z, mid, core, other) for other in others]

        def act():
            arrive(whole, across, 0)
            for target in beside_to:
                push(head, across, 0, target, cond)
            push(whole, across, 0, core_to, cond)
            for index in beside:
                arrive(whole, index, 0)
                push(tail, index, 1, across_to, cond)
                push(whole, index, 0, core_to, cond)

        guarded(cond, act)

    def stage_three(cond, z):
        diagonal = [slot(z, 1 - mid, core, other) for other in others]

        def act():
            for index in diagonal:
                arrive(head, index, 0)
                arrive(tail, index, 1)
                push(whole, index, 0, core_to, cond)

        guarded(cond, act)

    blocks = [(None, at, 0)]
    for step in range(1, line):
        blocks.append((at >= step, at - step, 1))
        blocks.append((at + step < line, at + step, -1))
    groups = [blocks[:1]] + [blocks[n : n + 2] for n in range(1, len(blocks), 2)]
    for turn in range(len(groups) + 2):
        if turn < len(groups):
            for cond, z, kind in groups[turn]:
                stage_one(cond, z, kind)
        if 0 <= turn - 1 < len(groups):
            for cond, z, _ in groups[turn - 1]:
                stage_two(cond, z)
        if 0 <= turn - 2:
            for cond, z, _ in groups[turn - 2]:
                stage_three(cond, z)
    for z in range(line):
        for m in range(2):
            for b in range(n_gy):
                arrive(whole, slot(z, m, 1 - core, b), 0)
    for cond, make in started:
        guarded(cond, lambda make=make: make().wait_send())


def gather_all(block, number):
    n_gx, n_gy = lax.axis_size("gx"), lax.axis_size("gy")
    devices = n_gx * n_gy
    rows, lanes = block.shape
    line = n_gx // 4
    pushes = (2 * line - 1) * (2 + 2 + (n_gy - 1) * 5) + 8
    size = devices * rows * lanes * 4
    return pl.pallas_call(
        functools.partial(gather_kernel, n_gx, n_gy),
        out_shape=jax.ShapeDtypeStruct((devices, rows, lanes), jnp.float32),
        in_specs=[pl.BlockSpec(memory_space=pltpu.VMEM)],
        out_specs=pl.BlockSpec(memory_space=pltpu.VMEM),
        scratch_shapes=[
            pltpu.SemaphoreType.DMA((pushes,)),
            pltpu.SemaphoreType.DMA((devices, 2)),
        ],
        compiler_params=pltpu.CompilerParams(
            collective_id=number,
            has_side_effects=True,
            vmem_limit_bytes=max(16 * 2**20, size + 8 * 2**20),
        ),
        name="gather_rows",
    )(block)


def pad_rows(value, rows):
    return jnp.pad(value, ((0, rows - value.shape[0]), (0, 128 - value.shape[1])))


def silu_slope(values):
    logistic = jax.nn.sigmoid(values)
    return logistic * (1.0 + values * (1.0 - logistic))


def round_up(count, step):
    return (count + step - 1) // step * step


def body(
    positions,
    species,
    neighbours,
    face_sends,
    corner_sends,
    embed,
    radial,
    w_up,
    w_charge,
    kvec,
    kfilter,
    read,
):
    atoms = positions.shape[1]
    kinds, channels = embed.shape
    basis = radial.shape[1]
    n_gx, n_gy = lax.axis_size("gx"), lax.axis_size("gy")
    devices = n_gx * n_gy
    total_atoms = atoms * devices
    waves = kvec.shape[1]
    share = waves // devices
    gx, gy = lax.axis_index("gx"), lax.axis_index("gy")
    me = gx * n_gy + gy
    scale = 1.0 / math.sqrt(total_atoms * waves)
    kind_ids = jnp.arange(kinds, dtype=jnp.int32)

    sends = jnp.concatenate([face_sends.reshape(-1), corner_sends.reshape(-1)])
    halo = sends.shape[0]
    widths = [face_sends.shape[1]] * 4 + [corner_sends.shape[1]] * 4
    starts = [sum(widths[:n]) for n in range(8)]
    send_hot = (sends[None, :] == jnp.arange(atoms, dtype=jnp.int32)[:, None]).astype(jnp.float32)
    own_rows = jnp.concatenate([positions, species.astype(jnp.float32)[None]], axis=0)
    sent = jnp.dot(own_rows, send_hot, precision=lax.Precision.HIGHEST)
    packet = jnp.concatenate([own_rows, sent], axis=1).reshape(-1, 128)
    count = packet.shape[0]
    spread = gather_all(pad_rows(packet, round_up(count, 8)), 0)[:, :count]
    spread = spread.reshape(devices, 4, atoms + halo)
    pieces = [own_rows]
    for (step_x, step_y), start, width in zip(DIRS, starts, widths):
        other = lax.rem(gx + step_x + n_gx, n_gx) * n_gy + lax.rem(gy + step_y + n_gy, n_gy)
        piece = lax.dynamic_slice(spread, (other, 0, atoms + start), (1, 4, width))[0]
        shift = jnp.array([step_x * DOMAIN, step_y * DOMAIN, 0.0, 0.0], jnp.float32)
        pieces.append(piece + shift[:, None])
    ext = jnp.concatenate(pieces, axis=1)
    limit = ext.shape[1]
    ext_kind = jnp.round(ext[3]).astype(jnp.int32)
    ext_hot = (ext_kind[:, None] == kind_ids[None, :]).astype(jnp.float32)
    ext_feat = mm("es,sc->ec", ext_hot, embed)
    own_hot = (species[:, None] == kind_ids[None, :]).astype(jnp.float32)
    initial = ext_feat[:atoms]

    ids = jnp.arange(limit, dtype=jnp.int32)[:, None]
    named = jnp.sum((neighbours[:, None, :] == ids[None]).astype(jnp.float32), axis=0)
    offset = ext[:3, :, None] - positions[:, None, :]
    dist_sq = jnp.sum(offset * offset, axis=0)
    radius = jnp.sqrt(dist_sq + SOFTEN)
    inside = jnp.maximum(1.0 - dist_sq / (CUTOFF * CUTOFF), 0.0)
    centers = jnp.arange(basis, dtype=jnp.float32) * (CUTOFF / (basis - 1))
    away = radius[None] - centers[:, None, None]
    gauss = jnp.exp(-2.0 * jnp.square(away)) * named[None]
    pair = gauss * jnp.square(inside)[None]
    pairs = jnp.concatenate([pair[None], pair[None] * offset[:, None]], axis=0)
    sums = mm("dmei,ec->dmic", pairs, ext_feat)
    message = mm_scale(sums[0], radial[0]) / 4.0
    vector = mm_scale(sums[1:], radial[1]) / 20.0
    invariants = message + jnp.sum(jnp.square(vector), axis=0)
    activated = invariants * jax.nn.sigmoid(invariants)
    updated = initial + mm("id,dc->ic", activated, w_up)
    charges = mm("id,dc->ic", updated, w_charge)

    turns = kvec * (1.0 / (2.0 * math.pi))
    rows = jnp.arange(devices, dtype=jnp.int32)
    every_x = spread[:, 0, :atoms] + ((rows // n_gy).astype(jnp.float32) * DOMAIN)[:, None]
    every_y = spread[:, 1, :atoms] + ((rows % n_gy).astype(jnp.float32) * DOMAIN)[:, None]
    every_z = spread[:, 2, :atoms]
    every = [v.reshape(1, total_atoms) for v in (every_x, every_y, every_z)]
    mine = lax.dynamic_slice(turns, (0, me * share), (3, share))
    phase = mine[0][:, None] * every[0] + mine[1][:, None] * every[1] + mine[2][:, None] * every[2]
    share_trig = jnp.concatenate(cos_sin(phase), axis=0)
    own_x = positions[0] + gx.astype(jnp.float32) * DOMAIN
    own_y = positions[1] + gy.astype(jnp.float32) * DOMAIN
    phase = (
        turns[0][:, None] * own_x + turns[1][:, None] * own_y + turns[2][:, None] * positions[2]
    )
    own_cos, own_sin = cos_sin(phase)
    own_trig = jnp.stack(
        [own_cos.reshape(devices, share, atoms), own_sin.reshape(devices, share, atoms)], axis=1
    ).reshape(2 * waves, atoms)
    every_kind = jnp.round(spread[:, 3, :atoms]).astype(jnp.int32).reshape(1, total_atoms)
    every_hot = (every_kind == kind_ids[:, None]).astype(jnp.float32)
    share_kinds = mm("sn,kn->sk", every_hot, share_trig)

    act_all = gather_all(
        jnp.concatenate([activated, pad_rows(share_kinds, 8)], axis=0), 1
    )
    kinds_all = act_all[:, atoms : atoms + kinds, : 2 * share]
    act_all = act_all[:, :atoms].reshape(total_atoms, channels)
    factor_act = gather_all(mm("kn,nc->kc", share_trig, act_all), 2)
    factor = mm("dkc,ce->dke", factor_act, mm("ac,ce->ae", w_up, w_charge)) + mm(
        "dsk,sc->dkc", kinds_all, mm("sc,ce->se", embed, w_charge)
    )
    factor = factor.reshape(devices, 2, share, channels)
    filters = (scale * kfilter).reshape(devices, 1, share, channels)
    filtered = (filters * factor).reshape(2 * waves, channels)
    potential = mm("ki,kc->ic", own_trig, filtered)
    combined = updated + potential
    logistic = jax.nn.sigmoid(combined)
    activated_out = combined * logistic
    atom_energy = jnp.sum(activated_out * read[None], axis=1)
    grad_combined = read[None] * logistic * (1.0 + combined * (1.0 - logistic))
    read_part = jnp.sum(activated_out, axis=0, keepdims=True)
    slope_all = gather_all(
        jnp.concatenate([grad_combined, pad_rows(read_part, 8)], axis=0), 1
    )
    grad_read = jnp.sum(slope_all[:, atoms], axis=0)
    slope_all = slope_all[:, :atoms].reshape(total_atoms, channels)
    projected = gather_all(mm("kn,nc->kc", share_trig, slope_all), 2)
    projected = projected.reshape(devices, 2, share, channels)
    grad_filter = (scale * jnp.sum(factor * projected, axis=1)).reshape(waves, channels)
    grad_factor = (filters * projected).reshape(2 * waves, channels)
    grad_charges = mm("ki,kc->ic", own_trig, grad_factor)
    along = mm(
        "kc,ic->ki",
        jnp.concatenate([filtered, grad_factor], axis=1),
        jnp.concatenate([grad_combined, charges], axis=1),
    ).reshape(devices, 2, share, atoms)
    trig = own_trig.reshape(devices, 2, share, atoms)
    grad_phase = (trig[:, 0] * along[:, 1] - trig[:, 1] * along[:, 0]).reshape(waves, atoms)
    grad_global = mm("dk,ki->di", kvec, grad_phase)

    grad_updated = grad_combined + mm("ic,dc->id", grad_charges, w_charge)
    grad_inv = mm("ic,dc->id", grad_updated, w_up) * silu_slope(invariants)
    cross_act = mm("kd,kc->dc", factor_act.reshape(2 * waves, channels), grad_factor)
    cross_kind = mm(
        "sk,kc->sc", kinds_all.transpose(1, 0, 2).reshape(kinds, 2 * waves), grad_factor
    )
    grad_wcharge = mm("da,dc->ac", w_up, cross_act) + mm("sa,sc->ac", embed, cross_kind)
    grad_wup = mm("nd,nc->dc", act_all, slope_all) + mm("de,ce->dc", cross_act, w_charge)

    grad_message = grad_inv / 4.0
    grad_vector = grad_inv[None] * vector * (2.0 / 20.0)
    radial_zero = jnp.sum(grad_message[None] * sums[0], axis=1)
    radial_one = jnp.sum(grad_vector[:, None] * sums[1:], axis=(0, 2))
    weights = jnp.concatenate(
        [
            (grad_message[None] * radial[0][:, None, :])[None],
            grad_vector[:, None] * radial[1][None, :, None, :],
        ],
        axis=0,
    )
    grad_feat = mm("dmei,dmic->ec", pairs, weights)
    grad_pairs = mm("dmic,ec->dmei", weights, ext_feat)
    grad_pair = grad_pairs[0] + jnp.sum(offset[:, None] * grad_pairs[1:], axis=0)
    slope = gauss * (
        (-2.0 / (CUTOFF * CUTOFF)) * inside[None]
        - (2.0 * jnp.square(inside) / radius)[None] * away
    )
    grad_dist = jnp.sum(grad_pair * slope, axis=0)
    grad_offset = jnp.sum(pair[None] * grad_pairs[1:], axis=1) + 2.0 * offset * grad_dist[None]
    grad_coords = -jnp.sum(grad_offset, axis=1)
    grad_ext = jnp.sum(grad_offset, axis=2)
    table = mm("es,ec->sc", ext_hot, grad_feat) + mm("is,ic->sc", own_hot, grad_updated)

    packet = jnp.concatenate(
        [table, radial_zero, radial_one, grad_ext[:, atoms:].reshape(-1, 128)], axis=0
    )
    last = gather_all(pad_rows(packet, round_up(packet.shape[0], 8)), 3)
    base = kinds + 2 * basis
    reduced = jnp.sum(last[:, :base], axis=0)
    back = last[:, base : packet.shape[0]].reshape(devices, 3, halo)
    returns = []
    for (step_x, step_y), start, width in zip(DIRS, starts, widths):
        other = lax.rem(gx - step_x + n_gx, n_gx) * n_gy + lax.rem(gy - step_y + n_gy, n_gy)
        returns.append(lax.dynamic_slice(back, (other, 0, start), (1, 3, width))[0])
    returned = mm("dj,aj->da", jnp.concatenate(returns, axis=1), send_hot)
    forces = -(grad_coords + grad_ext[:, :atoms] + returned + grad_global)
    mean = 1.0 / total_atoms
    return (
        atom_energy,
        forces,
        reduced[:kinds] * mean,
        reduced[kinds:].reshape(2, basis, channels) * mean,
        grad_wup * mean,
        grad_wcharge * mean,
        grad_filter,
        grad_read * mean,
    )


def mm_scale(sums, weights):
    return jnp.sum(sums * weights[:, None, :], axis=-3)


def solution(mesh):
    return jax.shard_map(
        body,
        mesh=mesh,
        in_specs=(
            P(None, ("gx", "gy")),
            P(("gx", "gy")),
            P(None, ("gx", "gy")),
            P(None, ("gx", "gy")),
            P(None, ("gx", "gy")),
            P(),
            P(),
            P(),
            P(),
            P(),
            P(),
            P(),
        ),
        out_specs=(P(("gx", "gy")), P(None, ("gx", "gy")), P(), P(), P(), P(), P(), P()),
        check_vma=False,
    )
```

```python
import functools
import math

import jax
import jax.numpy as jnp
import numpy as np
from jax import lax
from jax.experimental import pallas as pl
from jax.experimental.pallas import tpu as pltpu
from jax.sharding import PartitionSpec as P

CUTOFF = 5.0
SOFTEN = 0.01
DOMAIN = 8.8
HIGH = lax.Precision.HIGH
MESH = pl.DeviceIdType.MESH
DIRS = ((1, 0), (-1, 0), (0, 1), (0, -1), (1, 1), (1, -1), (-1, 1), (-1, -1))


def turn_tables():
    grid = 0.5 * np.cos(np.pi * (np.arange(400) + 0.5) / 400)
    grid = grid[grid > 0]
    square = grid * grid
    powers = np.stack([square**n for n in range(9)], axis=1)
    sine = np.linalg.lstsq(powers[:, :8], np.sin(2 * np.pi * grid) / grid, rcond=None)[0]
    cosine = np.linalg.lstsq(powers, np.cos(2 * np.pi * grid), rcond=None)[0]
    return [float(np.float32(v)) for v in sine], [float(np.float32(v)) for v in cosine]


SIN_TABLE, COS_TABLE = turn_tables()


def cos_sin(turns):
    part = turns - jnp.round(turns)
    square = part * part
    sine = jnp.full_like(part, SIN_TABLE[-1])
    for value in SIN_TABLE[-2::-1]:
        sine = sine * square + value
    cosine = jnp.full_like(part, COS_TABLE[-1])
    for value in COS_TABLE[-2::-1]:
        cosine = cosine * square + value
    return cosine, sine * part


def mm(spec, left, right):
    return jnp.einsum(spec, left, right, precision=HIGH, preferred_element_type=jnp.float32)


def gather_kernel(n_gx, n_gy, relay, x_ref, out_ref, send_sem, recv_sem):
    rows = x_ref.shape[0]
    first = (rows // 2 + 7) // 8 * 8
    line = n_gx // 4
    gx = lax.axis_index("gx")
    gy = lax.axis_index("gy")
    at = gx // 4
    mid = gx // 2 % 2
    core = gx % 2
    started = []

    def slot(z, m, c, b):
        return (z * 4 + m * 2 + c) * n_gy + b

    def whole(index):
        return out_ref.at[index]

    def head(index):
        return out_ref.at[index, pl.ds(0, first)]

    def tail(index):
        return out_ref.at[index, pl.ds(first, rows - first)]

    def push(view, index, half, device):
        copy = pltpu.make_async_remote_copy(
            src_ref=view(index),
            dst_ref=view(index),
            send_sem=send_sem.at[len(started)],
            recv_sem=recv_sem.at[index, half],
            device_id=device,
            device_id_type=MESH,
        )
        copy.start()
        started.append(copy)

    def arrive(view, index, half):
        pltpu.make_async_copy(view(index), view(index), recv_sem.at[index, half]).wait()

    def device(z, m, c, b):
        return (z * 4 + m * 2 + c, b)

    low = 1 - at // (line // 2)
    place = at * low + (line - 1 - at) * (1 - low)
    line_order = []
    for turn in range(line - 1):
        other = turn + (turn + line - place) // line
        line_order.append(other * low + (line - 1 - other) * (1 - low))
    others = [lax.rem(gy + step, n_gy) for step in range(1, n_gy)]
    across_to = device(at, 1 - mid, core, gy)
    core_to = device(at, mid, 1 - core, gy)
    beside_to = [device(at, mid, core, other) for other in others]
    corner_to = [device(at, 1 - mid, core, other) for other in others]
    line_to = [device(z, mid, core, gy) for z in line_order]
    targets = line_to + [across_to] + beside_to + [core_to] + ([] if relay else corner_to)

    barrier = pltpu.get_barrier_semaphore()
    for target in targets:
        pl.semaphore_signal(barrier, inc=1, device_id=target, device_id_type=MESH)
    out_ref[slot(at, mid, core, gy)] = x_ref[...]
    pl.semaphore_wait(barrier, len(targets))

    for number, z in enumerate([at] + line_order):
        own = slot(z, mid, core, gy)
        if number == 0:
            for target in line_to:
                push(whole, own, 0, target)
        else:
            arrive(whole, own, 0)
        for target in [across_to] + beside_to + ([] if relay else corner_to):
            push(whole, own, 0, target)
        push(whole, own, 0, core_to)
    for z in [at] + line_order:
        across = slot(z, 1 - mid, core, gy)
        arrive(whole, across, 0)
        if relay:
            for target in beside_to:
                push(head, across, 0, target)
        push(whole, across, 0, core_to)
        for other in others:
            beside = slot(z, mid, core, other)
            arrive(whole, beside, 0)
            if relay:
                push(tail, beside, 1, across_to)
            push(whole, beside, 0, core_to)
        if not relay:
            for other in others:
                corner = slot(z, 1 - mid, core, other)
                arrive(whole, corner, 0)
                push(whole, corner, 0, core_to)
    if relay:
        for z in [at] + line_order:
            for other in others:
                corner = slot(z, 1 - mid, core, other)
                arrive(head, corner, 0)
                arrive(tail, corner, 1)
                push(whole, corner, 0, core_to)
    for z in range(line):
        for m in range(2):
            for b in range(n_gy):
                arrive(whole, slot(z, m, 1 - core, b), 0)
    for copy in started:
        copy.wait_send()


def gather_all(block, number):
    n_gx, n_gy = lax.axis_size("gx"), lax.axis_size("gy")
    devices = n_gx * n_gy
    rows, lanes = block.shape
    line = n_gx // 4
    pushes = line * (4 + 5 * n_gy)
    size = devices * rows * lanes * 4
    return pl.pallas_call(
        functools.partial(gather_kernel, n_gx, n_gy, rows >= 64),
        out_shape=jax.ShapeDtypeStruct((devices, rows, lanes), jnp.float32),
        in_specs=[pl.BlockSpec(memory_space=pltpu.VMEM)],
        out_specs=pl.BlockSpec(memory_space=pltpu.VMEM),
        scratch_shapes=[
            pltpu.SemaphoreType.DMA((pushes,)),
            pltpu.SemaphoreType.DMA((devices, 2)),
        ],
        compiler_params=pltpu.CompilerParams(
            collective_id=number,
            has_side_effects=True,
            vmem_limit_bytes=max(16 * 2**20, size + 8 * 2**20),
        ),
        name="gather_rows",
    )(block)


def pad_rows(value, rows):
    return jnp.pad(value, ((0, rows - value.shape[0]), (0, 128 - value.shape[1])))


def silu_slope(values):
    logistic = jax.nn.sigmoid(values)
    return logistic * (1.0 + values * (1.0 - logistic))


def round_up(count, step):
    return (count + step - 1) // step * step


def body(
    positions,
    species,
    neighbours,
    face_sends,
    corner_sends,
    embed,
    radial,
    w_up,
    w_charge,
    kvec,
    kfilter,
    read,
):
    atoms = positions.shape[1]
    kinds, channels = embed.shape
    basis = radial.shape[1]
    n_gx, n_gy = lax.axis_size("gx"), lax.axis_size("gy")
    devices = n_gx * n_gy
    total_atoms = atoms * devices
    waves = kvec.shape[1]
    share = waves // devices
    gx, gy = lax.axis_index("gx"), lax.axis_index("gy")
    me = gx * n_gy + gy
    scale = 1.0 / math.sqrt(total_atoms * waves)
    kind_ids = jnp.arange(kinds, dtype=jnp.int32)

    sends = jnp.concatenate([face_sends.reshape(-1), corner_sends.reshape(-1)])
    halo = sends.shape[0]
    widths = [face_sends.shape[1]] * 4 + [corner_sends.shape[1]] * 4
    starts = [sum(widths[:n]) for n in range(8)]
    send_hot = (sends[None, :] == jnp.arange(atoms, dtype=jnp.int32)[:, None]).astype(jnp.float32)
    own_rows = jnp.concatenate([positions, species.astype(jnp.float32)[None]], axis=0)
    sent = jnp.dot(own_rows, send_hot, precision=lax.Precision.HIGHEST)
    packet = jnp.concatenate([own_rows, sent], axis=1).reshape(-1, 128)
    count = packet.shape[0]
    spread = gather_all(pad_rows(packet, round_up(count, 8)), 0)[:, :count]
    spread = spread.reshape(devices, 4, atoms + halo)
    pieces = [own_rows]
    for (step_x, step_y), start, width in zip(DIRS, starts, widths):
        other = lax.rem(gx + step_x + n_gx, n_gx) * n_gy + lax.rem(gy + step_y + n_gy, n_gy)
        piece = lax.dynamic_slice(spread, (other, 0, atoms + start), (1, 4, width))[0]
        shift = jnp.array([step_x * DOMAIN, step_y * DOMAIN, 0.0, 0.0], jnp.float32)
        pieces.append(piece + shift[:, None])
    ext = jnp.concatenate(pieces, axis=1)
    limit = ext.shape[1]
    ext_kind = jnp.round(ext[3]).astype(jnp.int32)
    ext_hot = (ext_kind[:, None] == kind_ids[None, :]).astype(jnp.float32)
    ext_feat = mm("es,sc->ec", ext_hot, embed)
    own_hot = (species[:, None] == kind_ids[None, :]).astype(jnp.float32)
    initial = ext_feat[:atoms]

    ids = jnp.arange(limit, dtype=jnp.int32)[:, None]
    named = jnp.sum((neighbours[:, None, :] == ids[None]).astype(jnp.float32), axis=0)
    offset = ext[:3, :, None] - positions[:, None, :]
    dist_sq = jnp.sum(offset * offset, axis=0)
    radius = jnp.sqrt(dist_sq + SOFTEN)
    inside = jnp.maximum(1.0 - dist_sq / (CUTOFF * CUTOFF), 0.0)
    centers = jnp.arange(basis, dtype=jnp.float32) * (CUTOFF / (basis - 1))
    away = radius[None] - centers[:, None, None]
    gauss = jnp.exp(-2.0 * jnp.square(away)) * named[None]
    pair = gauss * jnp.square(inside)[None]
    pairs = jnp.concatenate([pair[None], pair[None] * offset[:, None]], axis=0)
    sums = mm("dmei,ec->dmic", pairs, ext_feat)
    message = mm_scale(sums[0], radial[0]) / 4.0
    vector = mm_scale(sums[1:], radial[1]) / 20.0
    invariants = message + jnp.sum(jnp.square(vector), axis=0)
    activated = invariants * jax.nn.sigmoid(invariants)
    updated = initial + mm("id,dc->ic", activated, w_up)
    charges = mm("id,dc->ic", updated, w_charge)

    turns = kvec * (1.0 / (2.0 * math.pi))
    rows = jnp.arange(devices, dtype=jnp.int32)
    every_x = spread[:, 0, :atoms] + ((rows // n_gy).astype(jnp.float32) * DOMAIN)[:, None]
    every_y = spread[:, 1, :atoms] + ((rows % n_gy).astype(jnp.float32) * DOMAIN)[:, None]
    every_z = spread[:, 2, :atoms]
    every = [v.reshape(1, total_atoms) for v in (every_x, every_y, every_z)]
    mine = lax.dynamic_slice(turns, (0, me * share), (3, share))
    phase = mine[0][:, None] * every[0] + mine[1][:, None] * every[1] + mine[2][:, None] * every[2]
    share_trig = jnp.concatenate(cos_sin(phase), axis=0)
    own_x = positions[0] + gx.astype(jnp.float32) * DOMAIN
    own_y = positions[1] + gy.astype(jnp.float32) * DOMAIN
    phase = (
        turns[0][:, None] * own_x + turns[1][:, None] * own_y + turns[2][:, None] * positions[2]
    )
    own_cos, own_sin = cos_sin(phase)
    own_trig = jnp.stack(
        [own_cos.reshape(devices, share, atoms), own_sin.reshape(devices, share, atoms)], axis=1
    ).reshape(2 * waves, atoms)
    every_kind = jnp.round(spread[:, 3, :atoms]).astype(jnp.int32).reshape(1, total_atoms)
    every_hot = (every_kind == kind_ids[:, None]).astype(jnp.float32)
    share_kinds = mm("sn,kn->sk", every_hot, share_trig)

    act_all = gather_all(
        jnp.concatenate([activated, pad_rows(share_kinds, 8)], axis=0), 1
    )
    kinds_all = act_all[:, atoms : atoms + kinds, : 2 * share]
    act_all = act_all[:, :atoms].reshape(total_atoms, channels)
    factor_act = gather_all(mm("kn,nc->kc", share_trig, act_all), 2)
    factor = mm("dkc,ce->dke", factor_act, mm("ac,ce->ae", w_up, w_charge)) + mm(
        "dsk,sc->dkc", kinds_all, mm("sc,ce->se", embed, w_charge)
    )
    factor = factor.reshape(devices, 2, share, channels)
    filters = (scale * kfilter).reshape(devices, 1, share, channels)
    filtered = (filters * factor).reshape(2 * waves, channels)
    potential = mm("ki,kc->ic", own_trig, filtered)
    combined = updated + potential
    logistic = jax.nn.sigmoid(combined)
    activated_out = combined * logistic
    atom_energy = jnp.sum(activated_out * read[None], axis=1)
    grad_combined = read[None] * logistic * (1.0 + combined * (1.0 - logistic))
    read_part = jnp.sum(activated_out, axis=0, keepdims=True)
    slope_all = gather_all(
        jnp.concatenate([grad_combined, pad_rows(read_part, 8)], axis=0), 1
    )
    grad_read = jnp.sum(slope_all[:, atoms], axis=0)
    slope_all = slope_all[:, :atoms].reshape(total_atoms, channels)
    projected = gather_all(mm("kn,nc->kc", share_trig, slope_all), 2)
    projected = projected.reshape(devices, 2, share, channels)
    grad_filter = (scale * jnp.sum(factor * projected, axis=1)).reshape(waves, channels)
    grad_factor = (filters * projected).reshape(2 * waves, channels)
    grad_charges = mm("ki,kc->ic", own_trig, grad_factor)
    along = mm(
        "kc,ic->ki",
        jnp.concatenate([filtered, grad_factor], axis=1),
        jnp.concatenate([grad_combined, charges], axis=1),
    ).reshape(devices, 2, share, atoms)
    trig = own_trig.reshape(devices, 2, share, atoms)
    grad_phase = (trig[:, 0] * along[:, 1] - trig[:, 1] * along[:, 0]).reshape(waves, atoms)
    grad_global = mm("dk,ki->di", kvec, grad_phase)

    grad_updated = grad_combined + mm("ic,dc->id", grad_charges, w_charge)
    grad_inv = mm("ic,dc->id", grad_updated, w_up) * silu_slope(invariants)
    cross_act = mm("kd,kc->dc", factor_act.reshape(2 * waves, channels), grad_factor)
    cross_kind = mm(
        "sk,kc->sc", kinds_all.transpose(1, 0, 2).reshape(kinds, 2 * waves), grad_factor
    )
    grad_wcharge = mm("da,dc->ac", w_up, cross_act) + mm("sa,sc->ac", embed, cross_kind)
    grad_wup = mm("nd,nc->dc", act_all, slope_all) + mm("de,ce->dc", cross_act, w_charge)

    grad_message = grad_inv / 4.0
    grad_vector = grad_inv[None] * vector * (2.0 / 20.0)
    radial_zero = jnp.sum(grad_message[None] * sums[0], axis=1)
    radial_one = jnp.sum(grad_vector[:, None] * sums[1:], axis=(0, 2))
    weights = jnp.concatenate(
        [
            (grad_message[None] * radial[0][:, None, :])[None],
            grad_vector[:, None] * radial[1][None, :, None, :],
        ],
        axis=0,
    )
    grad_feat = mm("dmei,dmic->ec", pairs, weights)
    grad_pairs = mm("dmic,ec->dmei", weights, ext_feat)
    grad_pair = grad_pairs[0] + jnp.sum(offset[:, None] * grad_pairs[1:], axis=0)
    slope = gauss * (
        (-2.0 / (CUTOFF * CUTOFF)) * inside[None]
        - (2.0 * jnp.square(inside) / radius)[None] * away
    )
    grad_dist = jnp.sum(grad_pair * slope, axis=0)
    grad_offset = jnp.sum(pair[None] * grad_pairs[1:], axis=1) + 2.0 * offset * grad_dist[None]
    grad_coords = -jnp.sum(grad_offset, axis=1)
    grad_ext = jnp.sum(grad_offset, axis=2)
    table = mm("es,ec->sc", ext_hot, grad_feat) + mm("is,ic->sc", own_hot, grad_updated)

    packet = jnp.concatenate(
        [table, radial_zero, radial_one, grad_ext[:, atoms:].reshape(-1, 128)], axis=0
    )
    last = gather_all(pad_rows(packet, round_up(packet.shape[0], 8)), 3)
    base = kinds + 2 * basis
    reduced = jnp.sum(last[:, :base], axis=0)
    back = last[:, base : packet.shape[0]].reshape(devices, 3, halo)
    returns = []
    for (step_x, step_y), start, width in zip(DIRS, starts, widths):
        other = lax.rem(gx - step_x + n_gx, n_gx) * n_gy + lax.rem(gy - step_y + n_gy, n_gy)
        returns.append(lax.dynamic_slice(back, (other, 0, start), (1, 3, width))[0])
    returned = mm("dj,aj->da", jnp.concatenate(returns, axis=1), send_hot)
    forces = -(grad_coords + grad_ext[:, :atoms] + returned + grad_global)
    mean = 1.0 / total_atoms
    return (
        atom_energy,
        forces,
        reduced[:kinds] * mean,
        reduced[kinds:].reshape(2, basis, channels) * mean,
        grad_wup * mean,
        grad_wcharge * mean,
        grad_filter,
        grad_read * mean,
    )


def mm_scale(sums, weights):
    return jnp.sum(sums * weights[:, None, :], axis=-3)


def solution(mesh):
    return jax.shard_map(
        body,
        mesh=mesh,
        in_specs=(
            P(None, ("gx", "gy")),
            P(("gx", "gy")),
            P(None, ("gx", "gy")),
            P(None, ("gx", "gy")),
            P(None, ("gx", "gy")),
            P(),
            P(),
            P(),
            P(),
            P(),
            P(),
            P(),
        ),
        out_specs=(P(("gx", "gy")), P(None, ("gx", "gy")), P(), P(), P(), P(), P(), P()),
        check_vma=False,
    )
```

```python
import functools
import math

import jax
import jax.numpy as jnp
import numpy as np
from jax import lax
from jax.experimental import pallas as pl
from jax.experimental.pallas import tpu as pltpu
from jax.sharding import PartitionSpec as P

CUTOFF = 5.0
SOFTEN = 0.01
DOMAIN = 8.8
HIGH = lax.Precision.HIGH
MESH = pl.DeviceIdType.MESH
DIRS = ((1, 0), (-1, 0), (0, 1), (0, -1), (1, 1), (1, -1), (-1, 1), (-1, -1))


def turn_tables():
    grid = 0.5 * np.cos(np.pi * (np.arange(400) + 0.5) / 400)
    grid = grid[grid > 0]
    square = grid * grid
    powers = np.stack([square**n for n in range(9)], axis=1)
    sine = np.linalg.lstsq(powers[:, :8], np.sin(2 * np.pi * grid) / grid, rcond=None)[0]
    cosine = np.linalg.lstsq(powers, np.cos(2 * np.pi * grid), rcond=None)[0]
    return [float(np.float32(v)) for v in sine], [float(np.float32(v)) for v in cosine]


SIN_TABLE, COS_TABLE = turn_tables()


def cos_sin(turns):
    part = turns - jnp.round(turns)
    square = part * part
    sine = jnp.full_like(part, SIN_TABLE[-1])
    for value in SIN_TABLE[-2::-1]:
        sine = sine * square + value
    cosine = jnp.full_like(part, COS_TABLE[-1])
    for value in COS_TABLE[-2::-1]:
        cosine = cosine * square + value
    return cosine, sine * part


def mm(spec, left, right):
    return jnp.einsum(spec, left, right, precision=HIGH, preferred_element_type=jnp.float32)


def gather_kernel(n_gx, n_gy, relay, x_ref, out_ref, send_sem, recv_sem):
    rows = x_ref.shape[0]
    first = (rows // 2 + 7) // 8 * 8
    line = n_gx // 4
    gx = lax.axis_index("gx")
    gy = lax.axis_index("gy")
    at = gx // 4
    mid = gx // 2 % 2
    core = gx % 2
    started = []

    def slot(z, m, c, b):
        return (z * 4 + m * 2 + c) * n_gy + b

    def whole(index):
        return out_ref.at[index]

    def head(index):
        return out_ref.at[index, pl.ds(0, first)]

    def tail(index):
        return out_ref.at[index, pl.ds(first, rows - first)]

    def push(view, index, half, device):
        copy = pltpu.make_async_remote_copy(
            src_ref=view(index),
            dst_ref=view(index),
            send_sem=send_sem.at[len(started)],
            recv_sem=recv_sem.at[index, half],
            device_id=device,
            device_id_type=MESH,
        )
        copy.start()
        started.append(copy)

    def arrive(view, index, half):
        pltpu.make_async_copy(view(index), view(index), recv_sem.at[index, half]).wait()

    def device(z, m, c, b):
        return (z * 4 + m * 2 + c, b)

    low = 1 - at // (line // 2)
    place = at * low + (line - 1 - at) * (1 - low)
    line_order = []
    for turn in range(line - 1):
        other = turn + (turn + line - place) // line
        line_order.append(other * low + (line - 1 - other) * (1 - low))
    others = [lax.rem(gy + step, n_gy) for step in range(1, n_gy)]
    across_to = device(at, 1 - mid, core, gy)
    core_to = device(at, mid, 1 - core, gy)
    beside_to = [device(at, mid, core, other) for other in others]
    corner_to = [device(at, 1 - mid, core, other) for other in others]
    line_to = [device(z, mid, core, gy) for z in line_order]
    targets = line_to + [across_to] + beside_to + [core_to] + ([] if relay else corner_to)

    barrier = pltpu.get_barrier_semaphore()
    for target in targets:
        pl.semaphore_signal(barrier, inc=1, device_id=target, device_id_type=MESH)
    out_ref[slot(at, mid, core, gy)] = x_ref[...]
    pl.semaphore_wait(barrier, len(targets))

    for number, z in enumerate([at] + line_order):
        own = slot(z, mid, core, gy)
        if number == 0:
            for target in line_to:
                push(whole, own, 0, target)
        else:
            arrive(whole, own, 0)
        for target in [across_to] + beside_to + ([] if relay else corner_to):
            push(whole, own, 0, target)
        push(whole, own, 0, core_to)
    for z in [at] + line_order:
        across = slot(z, 1 - mid, core, gy)
        arrive(whole, across, 0)
        if relay:
            for target in beside_to:
                push(head, across, 0, target)
        push(whole, across, 0, core_to)
        for other in others:
            beside = slot(z, mid, core, other)
            arrive(whole, beside, 0)
            if relay:
                push(tail, beside, 1, across_to)
            push(whole, beside, 0, core_to)
        if not relay:
            for other in others:
                corner = slot(z, 1 - mid, core, other)
                arrive(whole, corner, 0)
                push(whole, corner, 0, core_to)
    if relay:
        for z in [at] + line_order:
            for other in others:
                corner = slot(z, 1 - mid, core, other)
                arrive(head, corner, 0)
                arrive(tail, corner, 1)
                push(whole, corner, 0, core_to)
    for z in range(line):
        for m in range(2):
            for b in range(n_gy):
                arrive(whole, slot(z, m, 1 - core, b), 0)
    for copy in started:
        copy.wait_send()


def gather_all(block, number):
    n_gx, n_gy = lax.axis_size("gx"), lax.axis_size("gy")
    devices = n_gx * n_gy
    rows, lanes = block.shape
    line = n_gx // 4
    pushes = line * (4 + 5 * n_gy)
    size = devices * rows * lanes * 4
    return pl.pallas_call(
        functools.partial(gather_kernel, n_gx, n_gy, rows >= 64),
        out_shape=jax.ShapeDtypeStruct((devices, rows, lanes), jnp.float32),
        in_specs=[pl.BlockSpec(memory_space=pltpu.VMEM)],
        out_specs=pl.BlockSpec(memory_space=pltpu.VMEM),
        scratch_shapes=[
            pltpu.SemaphoreType.DMA((pushes,)),
            pltpu.SemaphoreType.DMA((devices, 2)),
        ],
        compiler_params=pltpu.CompilerParams(
            collective_id=number,
            has_side_effects=True,
            vmem_limit_bytes=max(16 * 2**20, size + 8 * 2**20),
        ),
        name="gather_rows",
    )(block)


def split(value):
    high = value.astype(jnp.bfloat16)
    return high, (value - high.astype(jnp.float32)).astype(jnp.bfloat16)


def dot3(left, right, dims):
    def one(a, b):
        return lax.dot_general(a, b, (dims, ((), ())), preferred_element_type=jnp.float32)

    return one(left[0], right[0]) + (one(left[0], right[1]) + one(left[1], right[0]))


NN = ((1,), (0,))
NT = ((1,), (1,))
TN = ((0,), (0,))


def pair_terms(ext_cols, own_rows, named, basis):
    offset = [ext_cols[:, d : d + 1] - own_rows[d : d + 1, :] for d in range(3)]
    dist_sq = offset[0] * offset[0] + offset[1] * offset[1] + offset[2] * offset[2]
    inverse = lax.rsqrt(dist_sq + SOFTEN)
    radius = (dist_sq + SOFTEN) * inverse
    inside = jnp.maximum(1.0 - dist_sq / (CUTOFF * CUTOFF), 0.0)
    away = [radius - m * (CUTOFF / (basis - 1)) for m in range(basis)]
    gauss = [jnp.exp(-2.0 * (a * a)) * named for a in away]
    return offset, inverse, inside, away, gauss


def edge_forward_kernel(
    basis, nbr_ref, ext_ref, feat_ref, own_ref, radial_ref, named_ref, sums_ref, vec_ref, inv_ref, pair_s
):
    limit, atoms = named_ref.shape
    slots = nbr_ref.shape[0]
    chunk = 64
    for start in range(0, limit, chunk):
        ids = lax.broadcasted_iota(jnp.int32, (chunk, atoms), 0) + start
        count = jnp.zeros((chunk, atoms), jnp.float32)
        for s in range(slots):
            count = count + jnp.where(nbr_ref[s : s + 1, :] == ids, 1.0, 0.0)
        named_ref[start : start + chunk, :] = count
        offset, _, inside, _, gauss = pair_terms(
            ext_ref[start : start + chunk, :], own_ref[...], count, basis
        )
        envelope = inside * inside
        for m in range(basis):
            pair = gauss[m] * envelope
            for d in range(4):
                value = pair if d == 0 else pair * offset[d - 1]
                high, low = split(value)
                at = (d * basis + m) * atoms
                pair_s[0, start : start + chunk, at : at + atoms] = high
                pair_s[1, start : start + chunk, at : at + atoms] = low
    feat = split(feat_ref[...])
    wide = basis * atoms
    columns = radial_ref[...]
    total = None
    for d in range(4):
        part = (pair_s[0, :, d * wide : (d + 1) * wide], pair_s[1, :, d * wide : (d + 1) * wide])
        sums = dot3(feat, part, TN)
        sums_ref[:, d * wide : (d + 1) * wide] = sums
        base = 0 if d == 0 else basis
        mixed = columns[:, base : base + 1] * sums[:, :atoms]
        for m in range(1, basis):
            mixed = mixed + columns[:, base + m : base + m + 1] * sums[:, m * atoms : (m + 1) * atoms]
        if d == 0:
            total = mixed * (1.0 / 4.0)
        else:
            mixed = mixed * (1.0 / 20.0)
            vec_ref[d - 1] = mixed
            total = total + mixed * mixed
    inv_ref[...] = total


def edge_forward(neighbours, ext_cols, feat, own_rows, radial_cols, basis):
    limit, atoms = feat.shape[0], own_rows.shape[1]
    channels = feat.shape[1]
    shape = lambda *dims: jax.ShapeDtypeStruct(dims, jnp.float32)
    vmem = pl.BlockSpec(memory_space=pltpu.VMEM)
    return pl.pallas_call(
        functools.partial(edge_forward_kernel, basis),
        out_shape=[
            shape(limit, atoms),
            shape(channels, 4 * basis * atoms),
            shape(3, channels, atoms),
            shape(channels, atoms),
        ],
        in_specs=[vmem] * 5,
        out_specs=[vmem] * 4,
        scratch_shapes=[pltpu.VMEM((2, limit, 4 * basis * atoms), jnp.bfloat16)],
        compiler_params=pltpu.CompilerParams(vmem_limit_bytes=40 * 2**20),
        name="edge_forward",
    )(neighbours, ext_cols, feat, own_rows, radial_cols)


def edge_backward_kernel(
    basis,
    ext_ref,
    feat_ref,
    own_ref,
    radial_ref,
    named_ref,
    sums_ref,
    vec_ref,
    grad_ref,
    radial_out,
    coords_out,
    ext_out,
    feat_out,
    weight_s,
    pair_s,
    grads_s,
):
    limit, atoms = named_ref.shape
    wide = basis * atoms
    columns = radial_ref[...]
    lane = lax.broadcasted_iota(jnp.int32, (grad_ref.shape[0], 128), 1)
    radial_grad = jnp.zeros((grad_ref.shape[0], 128), jnp.float32)
    one_sums = [None] * basis
    for d in range(4):
        if d == 0:
            factor = grad_ref[...] * (1.0 / 4.0)
        else:
            factor = grad_ref[...] * vec_ref[d - 1] * (2.0 / 20.0)
        base = 0 if d == 0 else basis
        for m in range(basis):
            at = d * wide + m * atoms
            high, low = split(factor * columns[:, base + m : base + m + 1])
            weight_s[0, :, at : at + atoms] = high
            weight_s[1, :, at : at + atoms] = low
            term = factor * sums_ref[:, at : at + atoms]
            if d == 0:
                column = jnp.sum(term, axis=1, keepdims=True)
                radial_grad = jnp.where(lane == m, column, radial_grad)
            else:
                one_sums[m] = term if d == 1 else one_sums[m] + term
    for m in range(basis):
        column = jnp.sum(one_sums[m], axis=1, keepdims=True)
        radial_grad = jnp.where(lane == basis + m, column, radial_grad)
    radial_out[...] = radial_grad
    chunk = 128
    coords = [jnp.zeros((1, atoms), jnp.float32) for _ in range(3)]
    weights = (weight_s[0], weight_s[1])
    for start in range(0, limit, chunk):
        rows = slice(start, start + chunk)
        feat = split(feat_ref[rows, :])
        for d in range(4):
            part = (weight_s[0, :, d * wide : (d + 1) * wide], weight_s[1, :, d * wide : (d + 1) * wide])
            grads_s[:, d * wide : (d + 1) * wide] = dot3(feat, part, NN)
        small = 64
        for inner in range(0, chunk, small):
            near = slice(start + inner, start + inner + small)
            here = slice(inner, inner + small)
            offset, inverse, inside, away, gauss = pair_terms(
                ext_ref[near, :], own_ref[...], named_ref[near, :], basis
            )
            envelope = inside * inside
            steep = (-2.0 / (CUTOFF * CUTOFF)) * inside
            bend = 2.0 * envelope * inverse
            grad_dist = jnp.zeros_like(inside)
            direct = [jnp.zeros_like(inside) for _ in range(3)]
            for m in range(basis):
                pair = gauss[m] * envelope
                grad_pair = grads_s[here, m * atoms : (m + 1) * atoms]
                for d in range(4):
                    at = d * wide + m * atoms
                    if d > 0:
                        grad_part = grads_s[here, at : at + atoms]
                        grad_pair = grad_pair + offset[d - 1] * grad_part
                        direct[d - 1] = direct[d - 1] + pair * grad_part
                    high, low = split(pair if d == 0 else pair * offset[d - 1])
                    pair_s[0, here, at : at + atoms] = high
                    pair_s[1, here, at : at + atoms] = low
                grad_dist = grad_dist + grad_pair * gauss[m] * (steep - bend * away[m])
            for d in range(3):
                grad_offset = direct[d] + 2.0 * offset[d] * grad_dist
                coords[d] = coords[d] - jnp.sum(grad_offset, axis=0, keepdims=True)
                ext_out[near, d : d + 1] = jnp.sum(grad_offset, axis=1, keepdims=True)
        feat_out[rows, :] = dot3((pair_s[0], pair_s[1]), weights, NT)
    for d in range(3):
        coords_out[d : d + 1, :] = coords[d]


def edge_backward(ext_cols, feat, own_rows, radial_cols, named, sums, vector, grad_inv, basis):
    limit, atoms = named.shape
    channels = feat.shape[1]
    shape = lambda *dims: jax.ShapeDtypeStruct(dims, jnp.float32)
    vmem = pl.BlockSpec(memory_space=pltpu.VMEM)
    wide = 4 * basis * atoms
    return pl.pallas_call(
        functools.partial(edge_backward_kernel, basis),
        out_shape=[shape(channels, 128), shape(3, atoms), shape(limit, 3), shape(limit, channels)],
        in_specs=[vmem] * 8,
        out_specs=[vmem] * 4,
        scratch_shapes=[
            pltpu.VMEM((2, channels, wide), jnp.bfloat16),
            pltpu.VMEM((2, 128, wide), jnp.bfloat16),
            pltpu.VMEM((128, wide), jnp.float32),
        ],
        compiler_params=pltpu.CompilerParams(vmem_limit_bytes=40 * 2**20),
        name="edge_backward",
    )(ext_cols, feat, own_rows, radial_cols, named, sums, vector, grad_inv)


def pad_rows(value, rows):
    return jnp.pad(value, ((0, rows - value.shape[0]), (0, 128 - value.shape[1])))


def silu_slope(values):
    logistic = jax.nn.sigmoid(values)
    return logistic * (1.0 + values * (1.0 - logistic))


def round_up(count, step):
    return (count + step - 1) // step * step


def body(
    positions,
    species,
    neighbours,
    face_sends,
    corner_sends,
    embed,
    radial,
    w_up,
    w_charge,
    kvec,
    kfilter,
    read,
):
    atoms = positions.shape[1]
    kinds, channels = embed.shape
    basis = radial.shape[1]
    n_gx, n_gy = lax.axis_size("gx"), lax.axis_size("gy")
    devices = n_gx * n_gy
    total_atoms = atoms * devices
    waves = kvec.shape[1]
    share = waves // devices
    gx, gy = lax.axis_index("gx"), lax.axis_index("gy")
    me = gx * n_gy + gy
    scale = 1.0 / math.sqrt(total_atoms * waves)
    kind_ids = jnp.arange(kinds, dtype=jnp.int32)

    sends = jnp.concatenate([face_sends.reshape(-1), corner_sends.reshape(-1)])
    halo = sends.shape[0]
    widths = [face_sends.shape[1]] * 4 + [corner_sends.shape[1]] * 4
    starts = [sum(widths[:n]) for n in range(8)]
    send_hot = (sends[None, :] == jnp.arange(atoms, dtype=jnp.int32)[:, None]).astype(jnp.float32)
    own_rows = jnp.concatenate([positions, species.astype(jnp.float32)[None]], axis=0)
    sent = jnp.dot(own_rows, send_hot, precision=lax.Precision.HIGHEST)
    packet = jnp.concatenate([own_rows, sent], axis=1).reshape(-1, 128)
    count = packet.shape[0]
    spread = gather_all(pad_rows(packet, round_up(count, 8)), 0)[:, :count]
    spread = spread.reshape(devices, 4, atoms + halo)
    pieces = [own_rows]
    for (step_x, step_y), start, width in zip(DIRS, starts, widths):
        other = lax.rem(gx + step_x + n_gx, n_gx) * n_gy + lax.rem(gy + step_y + n_gy, n_gy)
        piece = lax.dynamic_slice(spread, (other, 0, atoms + start), (1, 4, width))[0]
        shift = jnp.array([step_x * DOMAIN, step_y * DOMAIN, 0.0, 0.0], jnp.float32)
        pieces.append(piece + shift[:, None])
    ext = jnp.concatenate(pieces, axis=1)
    limit = ext.shape[1]
    ext_kind = jnp.round(ext[3]).astype(jnp.int32)
    ext_hot = (ext_kind[:, None] == kind_ids[None, :]).astype(jnp.float32)
    ext_feat = mm("es,sc->ec", ext_hot, embed)
    own_hot = (species[:, None] == kind_ids[None, :]).astype(jnp.float32)
    initial = ext_feat[:atoms]

    ext_cols = ext.T
    radial_cols = radial.reshape(2 * basis, channels).T
    named, sums, vector, invariants = edge_forward(
        neighbours, ext_cols, ext_feat, positions, radial_cols, basis
    )
    invariants = invariants.T
    activated = invariants * jax.nn.sigmoid(invariants)
    updated = initial + mm("id,dc->ic", activated, w_up)
    charges = mm("id,dc->ic", updated, w_charge)

    turns = kvec * (1.0 / (2.0 * math.pi))
    rows = jnp.arange(devices, dtype=jnp.int32)
    every_x = spread[:, 0, :atoms] + ((rows // n_gy).astype(jnp.float32) * DOMAIN)[:, None]
    every_y = spread[:, 1, :atoms] + ((rows % n_gy).astype(jnp.float32) * DOMAIN)[:, None]
    every_z = spread[:, 2, :atoms]
    every = [v.reshape(1, total_atoms) for v in (every_x, every_y, every_z)]
    mine = lax.dynamic_slice(turns, (0, me * share), (3, share))
    phase = mine[0][:, None] * every[0] + mine[1][:, None] * every[1] + mine[2][:, None] * every[2]
    share_trig = jnp.concatenate(cos_sin(phase), axis=0)
    own_x = positions[0] + gx.astype(jnp.float32) * DOMAIN
    own_y = positions[1] + gy.astype(jnp.float32) * DOMAIN
    phase = (
        turns[0][:, None] * own_x + turns[1][:, None] * own_y + turns[2][:, None] * positions[2]
    )
    own_cos, own_sin = cos_sin(phase)
    own_trig = jnp.stack(
        [own_cos.reshape(devices, share, atoms), own_sin.reshape(devices, share, atoms)], axis=1
    ).reshape(2 * waves, atoms)
    every_kind = jnp.round(spread[:, 3, :atoms]).astype(jnp.int32).reshape(1, total_atoms)
    every_hot = (every_kind == kind_ids[:, None]).astype(jnp.float32)
    share_kinds = mm("sn,kn->sk", every_hot, share_trig)

    act_all = gather_all(
        jnp.concatenate([activated, pad_rows(share_kinds, 8)], axis=0), 1
    )
    kinds_all = act_all[:, atoms : atoms + kinds, : 2 * share]
    act_all = act_all[:, :atoms].reshape(total_atoms, channels)
    factor_act = gather_all(mm("kn,nc->kc", share_trig, act_all), 2)
    factor = mm("dkc,ce->dke", factor_act, mm("ac,ce->ae", w_up, w_charge)) + mm(
        "dsk,sc->dkc", kinds_all, mm("sc,ce->se", embed, w_charge)
    )
    factor = factor.reshape(devices, 2, share, channels)
    filters = (scale * kfilter).reshape(devices, 1, share, channels)
    filtered = (filters * factor).reshape(2 * waves, channels)
    potential = mm("ki,kc->ic", own_trig, filtered)
    combined = updated + potential
    logistic = jax.nn.sigmoid(combined)
    activated_out = combined * logistic
    atom_energy = jnp.sum(activated_out * read[None], axis=1)
    grad_combined = read[None] * logistic * (1.0 + combined * (1.0 - logistic))
    read_part = jnp.sum(activated_out, axis=0, keepdims=True)
    slope_all = gather_all(
        jnp.concatenate([grad_combined, pad_rows(read_part, 8)], axis=0), 1
    )
    grad_read = jnp.sum(slope_all[:, atoms], axis=0)
    slope_all = slope_all[:, :atoms].reshape(total_atoms, channels)
    projected = gather_all(mm("kn,nc->kc", share_trig, slope_all), 2)
    projected = projected.reshape(devices, 2, share, channels)
    grad_filter = (scale * jnp.sum(factor * projected, axis=1)).reshape(waves, channels)
    grad_factor = (filters * projected).reshape(2 * waves, channels)
    grad_charges = mm("ki,kc->ic", own_trig, grad_factor)
    along = mm(
        "kc,ic->ki",
        jnp.concatenate([filtered, grad_factor], axis=1),
        jnp.concatenate([grad_combined, charges], axis=1),
    ).reshape(devices, 2, share, atoms)
    trig = own_trig.reshape(devices, 2, share, atoms)
    grad_phase = (trig[:, 0] * along[:, 1] - trig[:, 1] * along[:, 0]).reshape(waves, atoms)
    grad_global = mm("dk,ki->di", kvec, grad_phase)

    grad_updated = grad_combined + mm("ic,dc->id", grad_charges, w_charge)
    grad_inv = mm("ic,dc->id", grad_updated, w_up) * silu_slope(invariants)
    cross_act = mm("kd,kc->dc", factor_act.reshape(2 * waves, channels), grad_factor)
    cross_kind = mm(
        "sk,kc->sc", kinds_all.transpose(1, 0, 2).reshape(kinds, 2 * waves), grad_factor
    )
    grad_wcharge = mm("da,dc->ac", w_up, cross_act) + mm("sa,sc->ac", embed, cross_kind)
    grad_wup = mm("nd,nc->dc", act_all, slope_all) + mm("de,ce->dc", cross_act, w_charge)

    radial_grad, grad_coords, grad_ext, grad_feat = edge_backward(
        ext_cols, ext_feat, positions, radial_cols, named, sums, vector, grad_inv.T, basis
    )
    grad_ext = grad_ext.T
    radial_grad = radial_grad[:, : 2 * basis].T
    table = mm("es,ec->sc", ext_hot, grad_feat) + mm("is,ic->sc", own_hot, grad_updated)

    packet = jnp.concatenate(
        [table, radial_grad, grad_ext[:, atoms:].reshape(-1, 128)], axis=0
    )
    last = gather_all(pad_rows(packet, round_up(packet.shape[0], 8)), 3)
    base = kinds + 2 * basis
    reduced = jnp.sum(last[:, :base], axis=0)
    back = last[:, base : packet.shape[0]].reshape(devices, 3, halo)
    returns = []
    for (step_x, step_y), start, width in zip(DIRS, starts, widths):
        other = lax.rem(gx - step_x + n_gx, n_gx) * n_gy + lax.rem(gy - step_y + n_gy, n_gy)
        returns.append(lax.dynamic_slice(back, (other, 0, start), (1, 3, width))[0])
    returned = mm("dj,aj->da", jnp.concatenate(returns, axis=1), send_hot)
    forces = -(grad_coords + grad_ext[:, :atoms] + returned + grad_global)
    mean = 1.0 / total_atoms
    return (
        atom_energy,
        forces,
        reduced[:kinds] * mean,
        reduced[kinds:].reshape(2, basis, channels) * mean,
        grad_wup * mean,
        grad_wcharge * mean,
        grad_filter,
        grad_read * mean,
    )


def solution(mesh):
    return jax.shard_map(
        body,
        mesh=mesh,
        in_specs=(
            P(None, ("gx", "gy")),
            P(("gx", "gy")),
            P(None, ("gx", "gy")),
            P(None, ("gx", "gy")),
            P(None, ("gx", "gy")),
            P(),
            P(),
            P(),
            P(),
            P(),
            P(),
            P(),
        ),
        out_specs=(P(("gx", "gy")), P(None, ("gx", "gy")), P(), P(), P(), P(), P(), P()),
        check_vma=False,
    )
```
